256 devices in a mesh: seq: 128 (over x, y, z), head: 2 (over core).
Axes of the slice: x: 4, y: 4, z: 8, core: 2. Of those that a mesh axis runs over, the one named last changes fastest.
Arguments:
- query_rows: bfloat16 [65536, 1024], P('seq', 'head'), may hold values from -16 to 16
- key_rows: bfloat16 [65536, 1024], P('seq', 'head'), may hold values from -16 to 16
- value_rows: bfloat16 [65536, 1024], P('seq', 'head'), may hold values from -16 to 16
- segment_lengths: int32 [256], replicated, may hold values from 1 to 512, 65536 in all
Outputs:
- attended: bfloat16 [65536, 1024], P('seq', 'head')
The draws below stay inside these ranges and needn't reach their ends.
Inputs may be any that keep to these rules, and one draw needn't show every extreme that they name: `segment_lengths`: they sum to 65536; the largest is exactly 512.
All inputs are finite; a program needn't handle non-finite values.
Results may differ from the reference program's by a relative error of at most 0.0065.
Values may be sent and summed in bfloat16 or wider, within the bound.
A program may use at most 192 MiB of HBM per device.

```python
import math
import jax
import jax.numpy as jnp
import numpy as np
from jax import lax

D = 1024
HEADS = 8
HEAD_DIM = 128
M = 256
ITERS = 6
TOK_DEV = 512
TOKENS = 65536
SEG_MOST = 512
N_SEQ = 128


def block_pattern(key, strength):
    span = TOKENS // (2 * M)
    blocks = -(-TOKENS // span)
    pattern = jnp.clip(jax.random.normal(key, (blocks, D), jnp.float32), -3.0, 3.0) * strength
    return jnp.repeat(pattern, span, axis=0)[:TOKENS]


def shared_parts(key):
    base = block_pattern(jax.random.fold_in(key, 101), math.sqrt(11.0 / math.sqrt(HEAD_DIM)))
    return base


def draw_query_rows(key, part):
    base = shared_parts(key)
    key = jax.random.fold_in(key, 1)
    rows = 0.7 * jax.random.normal(key, (TOKENS, D), jnp.float32) + base
    return jnp.clip(rows, -16.0, 16.0).astype(jnp.bfloat16)


def draw_key_rows(key, part):
    base = shared_parts(key)
    key = jax.random.fold_in(key, 2)
    rows = 0.7 * jax.random.normal(key, (TOKENS, D), jnp.float32) + base
    return jnp.clip(rows, -16.0, 16.0).astype(jnp.bfloat16)


def draw_value_rows(key, part):
    key = jax.random.fold_in(key, 3)
    first, second = jax.random.split(key, 2)
    pattern = block_pattern(first, 1.0)
    rows = 0.7 * jax.random.normal(second, (TOKENS, D), jnp.float32) + pattern
    return jnp.clip(rows, -16.0, 16.0).astype(jnp.bfloat16)


def length_profile(count, total, reach, skew):
    weights = [(1 << 20) // math.isqrt(rank ** skew) + 1 for rank in range(2, count + 1)]
    rest, given = total - reach - (count - 1), [1] * (count - 1)
    while rest > 0:
        candidates = [i for i in range(count - 1) if given[i] < reach]
        pool, remaining = sum([weights[i] for i in candidates]), rest
        for i in candidates:
            more = min(reach - given[i], max(1, remaining * weights[i] // pool), rest)
            given[i] = given[i] + more
            rest = rest - more
    return np.array([reach] + given)


def ragged(rng, count, total, most, slope):
    if count == 2:
        one = jax.random.randint(rng, (), max(1, total - most), min(most, total - 1) + 1)
        return jnp.stack([one, total - one])
    tallies = jnp.asarray(length_profile(count, total, most, slope), jnp.int32)
    twos = (count - 1) // 2
    source_of, sink = tallies[1:1 + 2 * twos:2], tallies[2:2 + 2 * twos:2]
    room = jnp.minimum(source_of - 1, most - sink)
    moved = jax.random.randint(jax.random.fold_in(rng, 1), (twos,), 0, 1 << 20) % (room + 1)
    tallies = tallies.at[1:1 + 2 * twos:2].set(source_of - moved).at[2:2 + 2 * twos:2].set(sink + moved)
    return tallies[jax.random.permutation(jax.random.fold_in(rng, 2), count)]


def setup_inputs(seed: int = 0) -> dict:
    splits = jax.random.split(jax.random.key(seed), 5)
    return {
        "query_rows": draw_query_rows(jax.random.fold_in(splits[4], 71), 0),
        "key_rows": draw_key_rows(jax.random.fold_in(splits[4], 71), 0),
        "value_rows": draw_value_rows(jax.random.fold_in(splits[4], 71), 0),
        "segment_lengths": ragged(splits[3], M, TOKENS, SEG_MOST, 1).astype(jnp.int32),
    }


def newton(attention_kernel, peak):
    eye = jnp.eye(attention_kernel.shape[-1], dtype=jnp.float32)
    high = lax.Precision.HIGHEST
    inverse = jnp.swapaxes(attention_kernel, -1, -2) / peak
    for step in range(ITERS):
        prod = jnp.matmul(attention_kernel, inverse, precision=high)
        inner = 7.0 * eye - prod
        inner = 15.0 * eye - jnp.matmul(prod, inner, precision=high)
        inner = 13.0 * eye - jnp.matmul(prod, inner, precision=high)
        inverse = 0.25 * jnp.matmul(inverse, inner, precision=high)
    return inverse

def reference(query_rows, key_rows, value_rows, segment_lengths):
    score_scale = 1.0 / math.sqrt(HEAD_DIM)
    ends = jnp.cumsum(segment_lengths)
    position = jnp.arange(TOKENS, dtype=jnp.int32)
    segments = jnp.searchsorted(ends, position, side='right').astype(jnp.int32)
    counts = segment_lengths.astype(jnp.float32)[:, None]
    query_land = (jax.ops.segment_sum(query_rows.astype(jnp.float32), segments, num_segments=M) / counts).astype(jnp.bfloat16)
    key_land = (jax.ops.segment_sum(key_rows.astype(jnp.float32), segments, num_segments=M) / counts).astype(jnp.bfloat16)
    query_head_stack = query_land.reshape(M, HEADS, HEAD_DIM).transpose(1, 0, 2)
    key_head_stack = key_land.reshape(M, HEADS, HEAD_DIM).transpose(1, 0, 2)
    attention_kernel = jax.nn.softmax(jnp.einsum('rvx,rqx->rvq', query_head_stack.astype(jnp.float32), key_head_stack.astype(jnp.float32)) * score_scale, axis=-1)
    peak = jnp.max(lax.optimization_barrier(jnp.sum(attention_kernel, axis=1)))
    inverse = newton(attention_kernel, peak)
    all_query = query_rows.reshape(TOKENS, HEADS, HEAD_DIM).transpose(1, 0, 2)
    all_key = key_rows.reshape(TOKENS, HEADS, HEAD_DIM).transpose(1, 0, 2)
    all_value = value_rows.reshape(TOKENS, HEADS, HEAD_DIM).transpose(1, 0, 2)

    def key_side(items):
        landmark_query, keys_head, values_head = items

        def shard_part(pair):
            key_part, value_part = pair
            score = jnp.dot(landmark_query, key_part.T, preferred_element_type=jnp.float32) * score_scale
            top = lax.optimization_barrier(jnp.max(score, axis=1))
            attention_weight = jnp.exp(score - top[:, None])
            total = lax.optimization_barrier(jnp.sum(attention_weight, axis=1))
            numer = jnp.dot(attention_weight.astype(jnp.bfloat16), value_part, preferred_element_type=jnp.float32)
            return (top, total, numer)
        tops, totals, numers = lax.map(shard_part, (keys_head.reshape(N_SEQ, TOK_DEV, HEAD_DIM), values_head.reshape(N_SEQ, TOK_DEV, HEAD_DIM)))
        highest = lax.optimization_barrier(jnp.max(tops, axis=0))
        factor = jnp.exp(tops - highest[None, :])
        total = lax.optimization_barrier(jnp.sum(factor * totals, axis=0))
        numer = lax.optimization_barrier(jnp.sum(factor[:, :, None] * numers, axis=0))
        return numer / total[:, None]
    keyside = lax.map(key_side, (query_head_stack, all_key, all_value))
    pseudo_inverse_mixer = jnp.matmul(inverse, keyside, precision=lax.Precision.HIGHEST).astype(jnp.bfloat16)

    def token_side(items):
        query_head, landmark_key, mix_head = items
        score = jnp.dot(query_head, landmark_key.T, preferred_element_type=jnp.float32) * score_scale
        attention_weight = jax.nn.softmax(score, axis=-1).astype(jnp.bfloat16)
        return jnp.dot(attention_weight, mix_head, preferred_element_type=jnp.float32).astype(jnp.bfloat16)
    attended = lax.map(token_side, (all_query, key_head_stack, pseudo_inverse_mixer))
    return attended.transpose(1, 0, 2).reshape(TOKENS, D)
```

```python
import functools
import math

import jax
import jax.numpy as jnp
from jax import lax
from jax.experimental import pallas as pl
from jax.experimental.pallas import tpu as pltpu
from jax.sharding import PartitionSpec as P

HEAD_DIM = 128
ITERS = 6
MESH = pl.DeviceIdType.MESH
F32 = jnp.float32
BF16 = jnp.bfloat16
HIGH = lax.Precision.HIGHEST


def nt(a, b, precision=None):
    return lax.dot_general(
        a, b, (((1,), (1,)), ((), ())), precision=precision, preferred_element_type=F32
    )


def nn(a, b, precision=None):
    return lax.dot_general(
        a, b, (((1,), (0,)), ((), ())), precision=precision, preferred_element_type=F32
    )


class Exchange:
    def __init__(self, n, me, seq_of, src, dst, send_sem, recv_sem):
        self.n, self.me, self.seq_of = n, me, seq_of
        self.src, self.dst = src, dst
        self.send_sem, self.recv_sem = send_sem, recv_sem

    def copy(self, partner, slot):
        return pltpu.make_async_remote_copy(
            src_ref=self.src(partner),
            dst_ref=self.dst(slot),
            send_sem=self.send_sem.at[partner],
            recv_sem=self.recv_sem.at[slot],
            device_id={"seq": self.seq_of(partner)},
            device_id_type=MESH,
        )

    def each(self, act):
        def body(i, carry):
            act(lax.rem(self.me + i, self.n))
            return carry

        lax.fori_loop(1, self.n, body, 0)

    def start(self):
        self.each(lambda p: self.copy(p, self.me).start())

    def start_one(self, p):
        @pl.when(p != self.me)
        def _():
            self.copy(p, self.me).start()

    def wait_recv(self):
        self.each(lambda p: self.copy(p, p).wait_recv())

    def wait_send(self):
        self.each(lambda p: self.copy(p, self.me).wait_send())


def kernel(
    n_plane, n_z,
    lens_ref, q_ref, k_ref, v_ref, out_ref,
    tail, sums_send, sums_recv, z_send, z_recv, land, peaks,
    numer_send, numer_recv, numer_z_send, numer_z_recv, mixer_z, mixer,
    kernel_ref, kernel_t, inv_ref, tok_weight,
    tail_sem, peak_sem,
    a_send, a_recv, b_send, b_recv, c_send, c_recv, d_send, d_recv,
    e_send, e_recv, f_send, f_recv, g_send, g_recv, h_send, h_recv,
):
    n_seq = n_plane * n_z
    toks, feats = q_ref.shape
    heads = feats // HEAD_DIM
    marks = lens_ref.shape[1]
    scale = 1.0 / math.sqrt(HEAD_DIM)
    mark_part = marks // n_plane
    col_part = 2 * feats // n_z
    row_part = feats // n_plane
    row_z = row_part // n_z
    parts_head = n_plane // heads

    seq = lax.axis_index("seq")
    head = lax.axis_index("head")
    plane, z = seq // n_z, lax.rem(seq, n_z)
    after, before = lax.rem(seq + 1, n_seq), lax.rem(seq + n_seq - 1, n_seq)

    def plane_seq(p):
        return p * n_z + z

    def z_seq(p):
        return plane * n_z + p

    barrier = pltpu.get_barrier_semaphore()

    def greet(**where):
        pl.semaphore_signal(barrier, inc=1, device_id=where, device_id_type=MESH)

    def greet_plane(i, carry):
        greet(seq=plane_seq(lax.rem(plane + i, n_plane)))
        return carry

    def greet_z(i, carry):
        greet(seq=z_seq(lax.rem(z + i, n_z)))
        return carry

    lax.fori_loop(1, n_plane, greet_plane, 0)
    lax.fori_loop(1, n_z, greet_z, 0)
    greet(seq=after)
    greet(seq=before)
    greet(head=1 - head)

    lens = lens_ref[...].astype(F32)
    row = lax.broadcasted_iota(jnp.int32, (marks, marks), 0)
    col = lax.broadcasted_iota(jnp.int32, (marks, marks), 1)
    counts = jnp.sum(jnp.where(col == row, lens, 0.0), axis=1, keepdims=True)
    ends = jnp.sum(jnp.where(col <= row, lens, 0.0), axis=1, keepdims=True)
    starts = ends - counts
    base = (seq * toks).astype(F32)
    top_pos = base + toks
    runs_on = (starts < top_pos) & (ends > top_pos)
    came_in = (starts < base) & (ends > base)
    run_start = top_pos + jnp.sum(jnp.where(runs_on, starts - top_pos, 0.0), axis=0, keepdims=True)

    pos8 = base + lax.broadcasted_iota(jnp.int32, (8, toks), 1).astype(F32)
    tail_member = jnp.where(pos8 >= run_start, 1.0, 0.0).astype(BF16)
    row8 = lax.broadcasted_iota(jnp.int32, (8, HEAD_DIM), 0)
    blocks = 2 * heads
    packed = jnp.zeros((8, HEAD_DIM), F32)
    for half, ref in enumerate((q_ref, k_ref)):
        sums = nn(tail_member, ref[...])
        for h in range(heads):
            packed = jnp.where(
                row8 == half * heads + h, sums[:, h * HEAD_DIM:(h + 1) * HEAD_DIM], packed
            )
    tail[0] = packed

    pl.semaphore_wait(barrier, (n_plane - 1) + (n_z - 1) + 3)
    tail_copy = pltpu.make_async_remote_copy(
        src_ref=tail.at[0], dst_ref=tail.at[1], send_sem=tail_sem.at[0], recv_sem=tail_sem.at[1],
        device_id={"seq": after}, device_id_type=MESH,
    )
    tail_copy.start()

    pos = base + lax.broadcasted_iota(jnp.int32, (marks, toks), 1).astype(F32)
    member = jnp.where((pos >= starts) & (pos < ends), 1.0, 0.0).astype(BF16)
    sums = [nn(member, q_ref[...]), nn(member, k_ref[...])]
    tail_copy.wait_recv()
    for b in range(blocks):
        s = sums[b // heads]
        o = (b % heads) * HEAD_DIM
        block = s[:, o:o + HEAD_DIM] + jnp.where(came_in, tail[1, b:b + 1, :], 0.0)
        block = jnp.where(runs_on, 0.0, block / counts).astype(BF16)
        sums_send[:, :, b * HEAD_DIM:(b + 1) * HEAD_DIM] = block.reshape(
            n_plane, mark_part, HEAD_DIM
        )

    ex_a = Exchange(n_plane, plane, plane_seq, lambda p: sums_send.at[p], lambda p: sums_recv.at[p],
                    a_send, a_recv)
    ex_a.start()
    sums_recv[plane] = sums_send[plane]
    ex_a.wait_recv()
    part = sums_recv[0].astype(F32)
    for p in range(1, n_plane):
        part = part + sums_recv[p].astype(F32)
    part = part.astype(BF16)
    for p in range(n_z):
        z_send[p] = part[:, p * col_part:(p + 1) * col_part]

    ex_b = Exchange(n_z, z, z_seq, lambda p: z_send.at[p], lambda p: z_recv.at[p], b_send, b_recv)
    ex_b.start()
    z_recv[z] = z_send[z]
    ex_b.wait_recv()
    part = z_recv[0].astype(F32)
    for p in range(1, n_z):
        part = part + z_recv[p].astype(F32)
    land[plane, z] = part.astype(BF16)

    ex_c = Exchange(n_z, z, z_seq, lambda p: land.at[plane, z], lambda p: land.at[plane, p],
                    c_send, c_recv)
    ex_c.start()
    ex_c.wait_recv()
    ex_d = Exchange(n_plane, plane, plane_seq, lambda p: land.at[plane], lambda p: land.at[p],
                    d_send, d_recv)
    ex_d.start()
    ex_d.wait_recv()

    def landmark(b):
        where, off = (b * HEAD_DIM) // col_part, (b * HEAD_DIM) % col_part
        return land[:, where, :, off:off + HEAD_DIM].reshape(marks, HEAD_DIM)

    my_head = plane // parts_head
    peak = jnp.zeros((1, 1), F32)
    for h in range(heads):
        score = nt(landmark(h), landmark(heads + h)) * scale
        weight = jnp.exp(score - jnp.max(score, axis=1, keepdims=True))
        soft = weight / jnp.sum(weight, axis=1, keepdims=True)
        column = jnp.sum(soft, axis=0, keepdims=True)
        peak = jnp.maximum(peak, jnp.max(column, axis=1, keepdims=True))

        @pl.when(my_head == h)
        def _():
            kernel_ref[...] = soft

    peaks[0] = jnp.broadcast_to(peak, (8, HEAD_DIM))
    peak_copy = pltpu.make_async_remote_copy(
        src_ref=peaks.at[0], dst_ref=peaks.at[1], send_sem=peak_sem.at[0], recv_sem=peak_sem.at[1],
        device_id={"head": 1 - head}, device_id_type=MESH,
    )
    peak_copy.start()

    ex_e = Exchange(n_plane, plane, plane_seq, lambda p: numer_send.at[p],
                    lambda p: numer_recv.at[p], e_send, e_recv)
    pad = numer_send.shape[1] - row_part - 2
    for h in range(heads):
        cols = slice(h * HEAD_DIM, (h + 1) * HEAD_DIM)
        score = nt(k_ref[:, cols], landmark(h)) * scale
        top = jnp.max(score, axis=0, keepdims=True)
        weight = jnp.exp(score - top)
        total = jnp.sum(weight, axis=0, keepdims=True)
        numer = lax.dot_general(
            v_ref[:, cols], weight.astype(BF16), (((0,), (0,)), ((), ())),
            preferred_element_type=F32,
        )
        for j in range(parts_head):
            p = h * parts_head + j
            numer_send[p, :row_part, :] = numer[j * row_part:(j + 1) * row_part]
            numer_send[p, row_part:row_part + 1, :] = top
            numer_send[p, row_part + 1:row_part + 2, :] = total
            numer_send[p, row_part + 2:, :] = jnp.zeros((pad, marks), F32)
            ex_e.start_one(p)
    numer_recv[plane] = numer_send[plane]

    kernel_t[...] = kernel_ref[...].T
    peak_copy.wait_recv()
    peak = jnp.maximum(peaks[0, 0:1, 0:1], peaks[1, 0:1, 0:1])
    inv_ref[...] = kernel_ref[...] / peak

    def newton(step, carry):
        inv = inv_ref[...]
        prod = nn(inv, kernel_t[...], HIGH)
        square = nn(prod, prod, HIGH)
        once = nn(prod, inv, HIGH)
        rest = nn(7.0 * prod - square, once, HIGH)
        inv_ref[...] = 0.25 * (13.0 * inv - 15.0 * once + rest)
        return carry

    lax.fori_loop(0, ITERS // 2, newton, 0)

    def merge(ref, count, rows):
        tops = [ref[p, rows:rows + 1, :] for p in range(count)]
        high = functools.reduce(jnp.maximum, tops)
        numer, total = None, None
        for p in range(count):
            factor = jnp.exp(tops[p] - high)
            n, t = factor * ref[p, :rows, :], factor * ref[p, rows + 1:rows + 2, :]
            numer, total = (n, t) if numer is None else (numer + n, total + t)
        return numer, total, high

    ex_e.wait_recv()
    numer, total, high = merge(numer_recv, n_plane, row_part)
    pad = numer_z_send.shape[1] - row_z - 2
    for p in range(n_z):
        numer_z_send[p, :row_z, :] = numer[p * row_z:(p + 1) * row_z]
        numer_z_send[p, row_z:row_z + 1, :] = high
        numer_z_send[p, row_z + 1:row_z + 2, :] = total
        numer_z_send[p, row_z + 2:, :] = jnp.zeros((pad, marks), F32)
    ex_f = Exchange(n_z, z, z_seq, lambda p: numer_z_send.at[p], lambda p: numer_z_recv.at[p],
                    f_send, f_recv)
    ex_f.start()
    numer_z_recv[z] = numer_z_send[z]

    lax.fori_loop(ITERS // 2, ITERS, newton, 0)

    ex_f.wait_recv()
    numer, total, high = merge(numer_z_recv, n_z, row_z)
    keyside = numer / total
    rows_z = mixer_z.shape[1]
    if rows_z > row_z:
        keyside = jnp.concatenate([keyside, jnp.zeros((rows_z - row_z, marks), F32)], axis=0)
    mixer_z[z] = nn(keyside, inv_ref[...], HIGH)
    ex_g = Exchange(n_z, z, z_seq, lambda p: mixer_z.at[z], lambda p: mixer_z.at[p], g_send, g_recv)
    ex_g.start()

    def token_side(h):
        score = nt(q_ref[:, h * HEAD_DIM:(h + 1) * HEAD_DIM], landmark(heads + h)) * scale
        weight = jnp.exp(score - jnp.max(score, axis=1, keepdims=True))
        tok_weight[h] = (weight / jnp.sum(weight, axis=1, keepdims=True)).astype(BF16)

    for h in range(heads // 2):
        token_side(h)
    ex_g.wait_recv()
    mixer[plane] = jnp.concatenate([mixer_z[p, :row_z, :] for p in range(n_z)], axis=0).astype(BF16)
    ex_h = Exchange(n_plane, plane, plane_seq, lambda p: mixer.at[plane], lambda p: mixer.at[p],
                    h_send, h_recv)
    ex_h.start()
    for h in range(heads // 2, heads):
        token_side(h)
    ex_h.wait_recv()
    for h in range(heads):
        mix = mixer[h * parts_head:(h + 1) * parts_head].reshape(HEAD_DIM, marks)
        out_ref[:, h * HEAD_DIM:(h + 1) * HEAD_DIM] = nt(tok_weight[h], mix).astype(BF16)

    tail_copy.wait_send()
    peak_copy.wait_send()
    for ex in (ex_a, ex_b, ex_c, ex_d, ex_e, ex_f, ex_g, ex_h):
        ex.wait_send()


def per_device(n_plane, n_z, query_rows, key_rows, value_rows, segment_lengths):
    toks, feats = query_rows.shape
    marks = segment_lengths.shape[0]
    heads = feats // HEAD_DIM
    mark_part, col_part = marks // n_plane, 2 * feats // n_z
    row_part = feats // n_plane
    row_z = row_part // n_z
    up = lambda n: -(-n // 8) * 8
    dma = pltpu.SemaphoreType.DMA
    return pl.pallas_call(
        functools.partial(kernel, n_plane, n_z),
        out_shape=jax.ShapeDtypeStruct((toks, feats), BF16),
        in_specs=[pl.BlockSpec(memory_space=pltpu.VMEM)] * 4,
        out_specs=pl.BlockSpec(memory_space=pltpu.VMEM),
        scratch_shapes=[
            pltpu.VMEM((2, 8, HEAD_DIM), F32),
            pltpu.VMEM((n_plane, mark_part, 2 * feats), BF16),
            pltpu.VMEM((n_plane, mark_part, 2 * feats), BF16),
            pltpu.VMEM((n_z, mark_part, col_part), BF16),
            pltpu.VMEM((n_z, mark_part, col_part), BF16),
            pltpu.VMEM((n_plane, n_z, mark_part, col_part), BF16),
            pltpu.VMEM((2, 8, HEAD_DIM), F32),
            pltpu.VMEM((n_plane, up(row_part + 2), marks), F32),
            pltpu.VMEM((n_plane, up(row_part + 2), marks), F32),
            pltpu.VMEM((n_z, up(row_z + 2), marks), F32),
            pltpu.VMEM((n_z, up(row_z + 2), marks), F32),
            pltpu.VMEM((n_z, up(row_z), marks), F32),
            pltpu.VMEM((n_plane, row_part, marks), BF16),
            pltpu.VMEM((marks, marks), F32),
            pltpu.VMEM((marks, marks), F32),
            pltpu.VMEM((marks, marks), F32),
            pltpu.VMEM((heads, toks, marks), BF16),
            dma((2,)),
            dma((2,)),
        ] + [dma((n,)) for n in (n_plane, n_z, n_z, n_plane, n_plane, n_z, n_z, n_plane) for _ in range(2)],
        compiler_params=pltpu.CompilerParams(
            collective_id=0, has_side_effects=True, vmem_limit_bytes=48 * 1024 * 1024
        ),
    )(segment_lengths.reshape(1, marks), query_rows, key_rows, value_rows)


def solution(mesh):
    n_seq = mesh.shape["seq"]
    n_z = 8 if n_seq >= 128 else 2
    in_specs = (P("seq", "head"), P("seq", "head"), P("seq", "head"), P())
    return jax.shard_map(
        functools.partial(per_device, n_seq // n_z, n_z),
        mesh=mesh, in_specs=in_specs, out_specs=P("seq", "head"), check_vma=False,
    )
```
